512 devices in a mesh: frame: 16 (over x, z_lo), row: 8 (over z_hi, core), col: 4 (over y).
Axes of the slice: x: 4, y: 4, z: 16 (z_hi: 4, z_lo: 4; z = z_hi * 4 + z_lo), core: 2. Of those that a mesh axis runs over, the one named last changes fastest.
Arguments:
- query: bfloat16 [2048, 128, 640], P(('frame', 'row'), 'col'), parts along dimension 0, may hold values from -6 to 6, as said below
- keys: bfloat16 [2048, 128, 640], P(('frame', 'row'), 'col'), parts along dimension 0, may hold values from -6 to 6, as said below
- values: bfloat16 [2048, 128, 640], P(('frame', 'row'), 'col'), parts along dimension 0, may hold values from -6 to 6
- out_weight: bfloat16 [640, 1280], P(None, ('row', 'col')), may hold values from -0.25 to 0.25
Outputs:
- projected: bfloat16 [2048, 128, 1280], P(('frame', 'row'), 'col'), parts along dimension 0
The draws below stay inside these ranges and needn't reach their ends.
There are 16 independent parts, one for each index of `frame`. The reference program is written for one: setup_inputs(seed, part) draws one part's arguments, and reference() takes and returns one part's arrays. A program takes and returns all parts, laid end to end along the dimension named above; an argument that names none is the same for every part. Nothing has to cross between parts.
Inputs may be any that keep to these rules, and one draw needn't show every extreme that they name: `query`: entries are real numbers of order one. `keys`: entries are real numbers of order one.
All inputs are finite; a program needn't handle non-finite values.
Results may differ from the reference program's by a relative error of at most 0.0056.
Values may be sent and summed in bfloat16 or wider, within the bound.
No kernel may reach another device: no remote copies, remote signals or barrier semaphores. Data moves between devices by JAX's collectives and lax.ppermute only.
A program may use at most 64 MiB of HBM per device.

```python
import jax
import jax.numpy as jnp
from jax import lax

WIDTH = 1280
HEADS = 8
HDIM = 80
BLOCK = 16
CHANNELS = 640
ROWS = 128
COLS = 128


def draw_query(key, part):
    key = jax.random.fold_in(key, 11)
    result = jax.random.truncated_normal(key, -6.0, 6.0, (ROWS, COLS, HEADS * HDIM), jnp.float32)
    return result.astype(jnp.bfloat16)


def draw_keys(key, part):
    key = jax.random.fold_in(key, 23)
    result = jax.random.truncated_normal(key, -6.0, 6.0, (ROWS, COLS, HEADS * HDIM), jnp.float32)
    return result.astype(jnp.bfloat16)


def steps_of(own_key, extent, shards, low, high):
    def one(dim, parts):
        steps = jax.random.uniform(jax.random.fold_in(jax.random.fold_in(own_key, 6), dim), (parts,), jnp.float32, low / len(shards), high / len(shards))
        return jnp.repeat(jnp.exp(steps), extent[dim] // parts).reshape((-1,) + (1,) * (len(extent) - dim - 1))

    gain = one(*shards[0])
    for cut in shards[1:]:
        gain = gain * one(*cut)
    return gain


def noise(own_key, shape, scale, reach, split=(), kind=jnp.bfloat16):
    values = jax.random.normal(own_key, shape, jnp.float32) * scale
    if len(split) > 0:
        values = steps_of(own_key, shape, split, -0.22, 0.18) * values
    return jnp.clip(values, min=-reach, max=reach).astype(kind)


def setup_inputs(seed: int = 0, part: int = 0) -> dict:
    key_of = jax.random.split(jax.random.key(seed), 5)
    part_keys = jax.random.split(jax.random.fold_in(key_of[4], part), 5)
    query = draw_query(jax.random.fold_in(jax.random.fold_in(key_of[4], part), 71), part)
    keys = draw_keys(jax.random.fold_in(jax.random.fold_in(key_of[4], part), 71), part)
    values = noise(part_keys[2], (ROWS, COLS, CHANNELS), 1.0, 6.0, ((0, 8), (1, 4)))
    out_weight = noise(key_of[3], (CHANNELS, WIDTH), CHANNELS ** -0.5, 0.25, ((1, 32),))
    return dict(query=query, keys=keys, values=values, out_weight=out_weight)


def attend_block(query_block, key_block, value_block, upper_ok, left_ok):
    side = query_block.shape[0]
    chans = query_block.shape[2]
    q_heads = query_block.reshape(side * side, HEADS, HDIM).astype(jnp.float32)
    k_heads = key_block.reshape(4 * side * side, HEADS, HDIM).astype(jnp.float32)
    v_heads = value_block.reshape(4 * side * side, HEADS, HDIM).astype(jnp.float32)
    scores = jnp.einsum("qhd,khd->hqk", q_heads, k_heads) * (HDIM ** -0.5)
    place = jnp.arange(4 * side * side, dtype=jnp.int32)
    in_upper = (place // (2 * side)) < side
    in_left = (place % (2 * side)) < side
    valid = jnp.logical_and(jnp.logical_or(jnp.logical_not(in_upper), upper_ok),
                            jnp.logical_or(jnp.logical_not(in_left), left_ok))
    scores = jnp.where(valid[None, None, :], scores, jnp.float32(-1e30))
    largest = jnp.max(scores, axis=-1, keepdims=True)
    weight = jnp.exp(scores - largest)
    total = jnp.sum(weight, axis=-1)
    rounded = weight.astype(jnp.bfloat16)
    mixed = jnp.einsum("hqk,khd->qhd", rounded.astype(jnp.float32), v_heads)
    mixed = mixed / jnp.transpose(total)[:, :, None]
    return mixed.reshape(side * side, chans).astype(jnp.bfloat16)


def reference(query, keys, values, out_weight):
    grid_rows = ROWS // BLOCK
    grid_cols = COLS // BLOCK
    chans = query.shape[2]
    padded_k = jnp.pad(keys, ((BLOCK, 0), (BLOCK, 0), (0, 0)))
    padded_v = jnp.pad(values, ((BLOCK, 0), (BLOCK, 0), (0, 0)))

    def one_block(index):
        brow = index // grid_cols
        bcol = index % grid_cols
        zero = jnp.zeros((), jnp.int32)
        query_block = lax.dynamic_slice(query, (brow * BLOCK, bcol * BLOCK, zero), (BLOCK, BLOCK, chans))
        key_block = lax.dynamic_slice(padded_k, (brow * BLOCK, bcol * BLOCK, zero), (2 * BLOCK, 2 * BLOCK, chans))
        value_block = lax.dynamic_slice(padded_v, (brow * BLOCK, bcol * BLOCK, zero), (2 * BLOCK, 2 * BLOCK, chans))
        return attend_block(query_block, key_block, value_block, brow > 0, bcol > 0)

    attended = lax.map(one_block, jnp.arange(grid_rows * grid_cols, dtype=jnp.int32))
    flat = attended.reshape(grid_rows * grid_cols * BLOCK * BLOCK, chans)
    projected = jnp.dot(flat, out_weight, preferred_element_type=jnp.float32).astype(jnp.bfloat16)
    width = out_weight.shape[1]
    projected = projected.reshape(grid_rows, grid_cols, BLOCK, BLOCK, width)
    projected = jnp.transpose(projected, (0, 2, 1, 3, 4))
    return projected.reshape(ROWS, COLS, width)
```

```python
import functools
import math

import jax
import jax.numpy as jnp
from jax import lax
from jax.experimental import pallas as pl
from jax.experimental.pallas import tpu as pltpu
from jax.sharding import PartitionSpec as P

HEADS = 8
HDIM = 80
BLOCK = 16
TOKENS = BLOCK * BLOCK
CHANNELS = HEADS * HDIM
SCALE = math.log2(math.e) * HDIM ** (-0.5)
NEG = -1e30
PACKED = CHANNELS + 32
SIDE = 4
AXES = ("frame", "row", "col")


def routed(block, target):
    route = []
    for x in range(SIDE):
        for zl in range(SIDE):
            for zh in range(SIDE):
                for core in range(2):
                    for y in range(SIDE):
                        to = target(x, zl, zh, core, y)
                        if to is not None:
                            route.append((place(x, zl, zh, core, y), place(*to)))
    return lax.ppermute(block, AXES, route)


def place(x, zl, zh, core, y):
    return ((x * SIDE + zl) * 2 * SIDE + zh * 2 + core) * SIDE + y


def shifted(block, axis, distance):
    devices = range(lax.axis_size(axis))
    route = [(i - distance, i) for i in devices if i - distance in devices]
    return lax.ppermute(block, axis, route)


def head_scores(keys, query_t, head):
    first = head * HDIM
    low = first // 128 * 128
    high = -(-(first + HDIM) // 128) * 128
    parts = []
    if first > low:
        parts.append(jnp.zeros((first - low, TOKENS), jnp.bfloat16))
    parts.append(query_t[first : first + HDIM])
    if high > first + HDIM:
        parts.append(jnp.zeros((high - first - HDIM, TOKENS), jnp.bfloat16))
    masked = jnp.concatenate(parts, axis=0)
    return jnp.dot(keys[:, low:high], masked, preferred_element_type=jnp.float32)


def attend(query_t, keys_a, keys_b, values_a, values_b, bias, emit):
    for head in range(HEADS):
        rows = slice(head * HDIM, (head + 1) * HDIM)
        score_a = head_scores(keys_a, query_t, head)
        score_b = head_scores(keys_b, query_t, head)
        if bias is not None:
            score_a = score_a + bias
        largest = jnp.maximum(
            jnp.max(score_a, axis=0, keepdims=True), jnp.max(score_b, axis=0, keepdims=True)
        )
        largest = largest * SCALE
        weight_a = jnp.exp2(score_a * SCALE - largest)
        weight_b = jnp.exp2(score_b * SCALE - largest)
        total = jnp.sum(weight_a, axis=0, keepdims=True) + jnp.sum(weight_b, axis=0, keepdims=True)
        mixed = jnp.dot(
            values_a[rows], weight_a.astype(jnp.bfloat16), preferred_element_type=jnp.float32
        ) + jnp.dot(
            values_b[rows], weight_b.astype(jnp.bfloat16), preferred_element_type=jnp.float32
        )
        emit(head, rows, mixed, largest, total)


def block_of(ref, col):
    return ref[:, col * BLOCK : (col + 1) * BLOCK, :].reshape(TOKENS, CHANNELS)


def left_bias():
    return jnp.where(lax.axis_index("col") > 0, jnp.float32(0.0), jnp.float32(NEG))


def own_kernel(query, keys, values, mixed_out, stats_out, values_t):
    values_t[0] = block_of(values, 0).T
    values_t[1] = block_of(values, 1).T

    def emit(head, rows, mixed, largest, total):
        mixed_out[rows] = mixed
        stats_out[head : head + 1] = largest
        stats_out[HEADS + head : HEADS + head + 1] = total

    attend(
        block_of(query, 1).T, block_of(keys, 0), block_of(keys, 1),
        values_t.at[0], values_t.at[1], None, emit,
    )


def edge_kernel(query, keys, left, values_t, mixed_out, stats_out, left_t):
    left_t[...] = left[BLOCK:].reshape(TOKENS, CHANNELS).T

    def emit(head, rows, mixed, largest, total):
        mixed_out[rows] = mixed
        stats_out[head : head + 1] = largest
        stats_out[HEADS + head : HEADS + head + 1] = total

    attend(
        block_of(query, 0).T, left[:BLOCK].reshape(TOKENS, CHANNELS), block_of(keys, 0),
        left_t, values_t.at[0], left_bias(), emit,
    )


def packing(packed, lse):
    def emit(head, rows, mixed, largest, total):
        packed[rows] = (mixed * (1.0 / total)).astype(jnp.bfloat16)
        lse[head : head + 1] = largest + jnp.log2(total)

    return emit


def pack_lse(packed, lse):
    whole = lse[...]
    high = whole.astype(jnp.bfloat16)
    rest = whole - high.astype(jnp.float32)
    middle = rest.astype(jnp.bfloat16)
    low = (rest - middle.astype(jnp.float32)).astype(jnp.bfloat16)
    packed[CHANNELS : CHANNELS + 16] = jnp.concatenate(
        [high.astype(jnp.float32), middle.astype(jnp.float32)], axis=0
    ).astype(jnp.bfloat16)
    packed[CHANNELS + 16 : CHANNELS + 32] = jnp.concatenate(
        [low.astype(jnp.float32), jnp.zeros_like(whole)], axis=0
    ).astype(jnp.bfloat16)


def lower_own_kernel(query, keys, values_t, packed, lse):
    attend(
        block_of(query, 1).T, block_of(keys, 0), block_of(keys, 1),
        values_t.at[0], values_t.at[1], None, packing(packed, lse),
    )
    pack_lse(packed, lse)


def lower_edge_kernel(query, keys, left, values_t, left_t, packed, lse):
    attend(
        block_of(query, 0).T, left[:BLOCK].reshape(TOKENS, CHANNELS), block_of(keys, 0),
        left_t, values_t.at[0], left_bias(), packing(packed, lse),
    )
    pack_lse(packed, lse)


def project_kernel(
    mixed_0, mixed_1, stats_0, stats_1, upper_0, upper_1, weight, other, projected, full, merged
):
    frame, row = lax.axis_index("frame"), lax.axis_index("row")
    x, z_hi, core = frame // SIDE, row // 2, row % 2
    span = SIDE * weight.shape[0] // (SIDE * SIDE)
    for item in range(SIDE):
        holder = lax.rem(z_hi + lax.rem(x + item, SIDE), SIDE) * 2
        for source, which in ((weight, core), (other, 1 - core)):
            start = pl.multiple_of((holder + which) * span, span)
            full[pl.ds(start, span)] = source[item * span : (item + 1) * span]
    has_upper = row > 0
    for col, (mixed, stats, upper) in enumerate(
        ((mixed_0, stats_0, upper_0), (mixed_1, stats_1, upper_1))
    ):
        largest, total = stats[:HEADS], stats[HEADS:]
        parts = upper[CHANNELS : CHANNELS + 32].astype(jnp.float32)
        lse = parts[:HEADS] + parts[HEADS : 2 * HEADS] + parts[2 * HEADS : 3 * HEADS]
        lse = jnp.where(has_upper, lse, jnp.float32(NEG))
        top = jnp.maximum(largest, lse)
        own_w = jnp.exp2(largest - top)
        upper_w = jnp.exp2(lse - top)
        share = 1.0 / (total * own_w + upper_w)
        own_w, upper_w = own_w * share, upper_w * share
        for head in range(HEADS):
            rows = slice(head * HDIM, (head + 1) * HDIM)
            merged[rows] = (
                mixed[rows] * own_w[head : head + 1]
                + upper[rows].astype(jnp.float32) * upper_w[head : head + 1]
            ).astype(jnp.bfloat16)
        result = lax.dot_general(
            merged[...].T, full[...], (((1,), (1,)), ((), ())), preferred_element_type=jnp.float32
        )
        projected[:, col * BLOCK : (col + 1) * BLOCK, :] = result.astype(jnp.bfloat16).reshape(
            BLOCK, BLOCK, projected.shape[2]
        )


def call(kernel, outs, scratch=(), flops=0, name=None):
    return pl.pallas_call(
        kernel,
        out_shape=outs,
        scratch_shapes=list(scratch),
        compiler_params=pltpu.CompilerParams(vmem_limit_bytes=32 * 1024 * 1024),
        cost_estimate=pl.CostEstimate(flops=flops, bytes_accessed=4_000_000, transcendentals=0),
        name=name,
    )


def gathered_weight(shard):
    item = routed(shard, lambda x, zl, zh, c, y: (x, zl, (zh - x) % SIDE, c, y))
    turns = [item] + [
        routed(item, lambda x, zl, zh, c, y: (x, zl, zh, c, (y - j) % SIDE)) for j in range(1, SIDE)
    ]
    ring = jnp.concatenate(turns + turns[:-1], axis=0)
    start = lax.rem(SIDE - lax.axis_index("col"), SIDE) * shard.shape[0]
    quarter = lax.dynamic_slice_in_dim(ring, start, SIDE * shard.shape[0], axis=0)
    items = [quarter] + [
        routed(quarter, lambda x, zl, zh, c, y: ((x - j) % SIDE, zl, zh, c, y))
        for j in range(1, SIDE)
    ]
    half = jnp.concatenate(items, axis=0)
    return half, routed(half, lambda x, zl, zh, c, y: (x, zl, zh, 1 - c, y))


def on_device(query, keys, values, out_weight):
    rows_dev, cols_dev, chans = query.shape
    width = out_weight.shape[1] * lax.axis_size("row") * lax.axis_size("col")
    lower_query = shifted(query, "row", -1)
    left = shifted(
        jnp.concatenate([keys[:, -BLOCK:], values[:, -BLOCK:]], axis=0), "col", 1
    )
    weight, other = gathered_weight(out_weight.T)

    f32, bf16 = jnp.float32, jnp.bfloat16
    mixed_s = jax.ShapeDtypeStruct((CHANNELS, TOKENS), f32)
    stats_s = jax.ShapeDtypeStruct((2 * HEADS, TOKENS), f32)
    packed_s = jax.ShapeDtypeStruct((PACKED, TOKENS), bf16)
    lse = pltpu.VMEM((HEADS, TOKENS), f32)
    flops = 4 * HEADS * TOKENS * 2 * TOKENS * 256

    mixed_1, stats_1, values_t = call(
        own_kernel, (mixed_s, stats_s, jax.ShapeDtypeStruct((2, CHANNELS, TOKENS), bf16)),
        flops=flops, name="own",
    )(query, keys, values)
    mixed_0, stats_0, left_t = call(
        edge_kernel, (mixed_s, stats_s, jax.ShapeDtypeStruct((CHANNELS, TOKENS), bf16)),
        flops=flops, name="edge",
    )(query, keys, left, values_t)
    packed_1 = call(lower_own_kernel, packed_s, (lse,), flops=flops, name="lower_own")(
        lower_query, keys, values_t
    )
    upper_1 = shifted(packed_1, "row", 1)
    packed_0 = call(lower_edge_kernel, packed_s, (lse,), flops=flops, name="lower_edge")(
        lower_query, keys, left, values_t, left_t
    )
    upper_0 = shifted(packed_0, "row", 1)
    return call(
        project_kernel,
        jax.ShapeDtypeStruct((rows_dev, cols_dev, width), bf16),
        (pltpu.VMEM((width, chans), bf16), pltpu.VMEM((CHANNELS, TOKENS), bf16)),
        flops=2 * 2 * TOKENS * CHANNELS * width, name="project",
    )(mixed_0, mixed_1, stats_0, stats_1, upper_0, upper_1, weight, other)


def solution(mesh):
    placed = (
        P(("frame", "row"), "col", None),
        P(("frame", "row"), "col", None),
        P(("frame", "row"), "col", None),
        P(None, ("row", "col")),
    )
    return jax.shard_map(
        on_device,
        mesh=mesh,
        in_specs=placed,
        out_specs=P(("frame", "row"), "col", None),
        check_vma=False,
    )
```

```python
import functools
import math

import jax
import jax.numpy as jnp
from jax import lax
from jax.experimental import pallas as pl
from jax.experimental.pallas import tpu as pltpu
from jax.sharding import PartitionSpec as P

HEADS = 8
HDIM = 80
BLOCK = 16
TOKENS = BLOCK * BLOCK
CHANNELS = HEADS * HDIM
SCALE = math.log2(math.e) * HDIM ** (-0.5)
NEG = -1e30
PACKED = CHANNELS + 32
SIDE = 4
AXES = ("frame", "row", "col")


def place(x, zl, zh, core, y):
    return ((x * SIDE + zl) * 2 * SIDE + zh * 2 + core) * SIDE + y


def routed(block, members, target):
    route = []
    for x in range(SIDE):
        for zl in members:
            for zh in range(SIDE):
                for core in range(2):
                    for y in range(SIDE):
                        to = target(x, zh, core, y)
                        if to is not None:
                            route.append((place(x, zl, zh, core, y), place(to[0], zl, *to[1:])))
    return lax.ppermute(block, AXES, route)


def to_row(distance):
    def target(x, zh, core, y):
        row = zh * 2 + core + distance
        return (x, row // 2, row % 2, y) if 0 <= row < 2 * SIDE else None

    return target


def to_right(x, zh, core, y):
    return (x, zh, core, y + 1) if y + 1 < SIDE else None


def head_scores(keys, query_t, head):
    first = head * HDIM
    low = first // 128 * 128
    high = -(-(first + HDIM) // 128) * 128
    parts = []
    if first > low:
        parts.append(jnp.zeros((first - low, TOKENS), jnp.bfloat16))
    parts.append(query_t[first : first + HDIM])
    if high > first + HDIM:
        parts.append(jnp.zeros((high - first - HDIM, TOKENS), jnp.bfloat16))
    masked = jnp.concatenate(parts, axis=0)
    return jnp.dot(keys[:, low:high], masked, preferred_element_type=jnp.float32)


def attend(query_t, pair_a, pair_b, bias, emit):
    keys_a, keys_b = (p[:BLOCK].reshape(TOKENS, CHANNELS) for p in (pair_a, pair_b))
    values_a, values_b = (p[BLOCK:].reshape(TOKENS, CHANNELS).T for p in (pair_a, pair_b))
    for head in range(HEADS):
        rows = slice(head * HDIM, (head + 1) * HDIM)
        score_a = head_scores(keys_a, query_t, head)
        score_b = head_scores(keys_b, query_t, head)
        if bias is not None:
            score_a = score_a + bias
        largest = jnp.maximum(
            jnp.max(score_a, axis=0, keepdims=True), jnp.max(score_b, axis=0, keepdims=True)
        )
        largest = largest * SCALE
        weight_a = jnp.exp2(score_a * SCALE - largest)
        weight_b = jnp.exp2(score_b * SCALE - largest)
        total = jnp.sum(weight_a, axis=0, keepdims=True) + jnp.sum(weight_b, axis=0, keepdims=True)
        mixed = jnp.dot(
            values_a[rows], weight_a.astype(jnp.bfloat16), preferred_element_type=jnp.float32
        ) + jnp.dot(
            values_b[rows], weight_b.astype(jnp.bfloat16), preferred_element_type=jnp.float32
        )
        emit(head, rows, mixed, largest, total)


def block_of(ref, col):
    return ref[:, col * BLOCK : (col + 1) * BLOCK, :].reshape(TOKENS, CHANNELS)


def edge_bias(col):
    if col > 0:
        return None
    return jnp.where(lax.axis_index("col") > 0, jnp.float32(0.0), jnp.float32(NEG))


def pair_kernel(keys, values, pair_0, pair_1):
    for col, pair in ((0, pair_0), (1, pair_1)):
        pair[:BLOCK] = keys[:, col * BLOCK : (col + 1) * BLOCK]
        pair[BLOCK:] = values[:, col * BLOCK : (col + 1) * BLOCK]


def stack_kernel(*refs):
    for j, ref in enumerate(refs[:-1]):
        refs[-1][j] = ref[...]


def own_kernel(col, query, pair_a, pair_b, mixed_out, stats_out):
    def emit(head, rows, mixed, largest, total):
        mixed_out[rows] = mixed
        stats_out[head : head + 1] = largest
        stats_out[HEADS + head : HEADS + head + 1] = total

    attend(block_of(query, col).T, pair_a, pair_b, edge_bias(col), emit)


def part_kernel(col, query, pair_a, pair_b, packed, lse):
    def emit(head, rows, mixed, largest, total):
        packed[rows] = (mixed * (1.0 / total)).astype(jnp.bfloat16)
        lse[head : head + 1] = largest + jnp.log2(total)

    attend(block_of(query, col).T, pair_a, pair_b, edge_bias(col), emit)
    whole = lse[...]
    high = whole.astype(jnp.bfloat16).astype(jnp.float32)
    middle = (whole - high).astype(jnp.bfloat16).astype(jnp.float32)
    low = whole - high - middle
    packed[CHANNELS : CHANNELS + 16] = jnp.concatenate([high, middle], axis=0).astype(jnp.bfloat16)
    packed[CHANNELS + 16 : CHANNELS + 32] = jnp.concatenate(
        [low, jnp.zeros_like(whole)], axis=0
    ).astype(jnp.bfloat16)


def order_kernel(weight, other, full):
    row = lax.axis_index("row")
    z_hi, core = row // 2, row % 2
    span = full.shape[0] // (2 * SIDE)
    for item in range(SIDE):
        holder = lax.rem(z_hi + item, SIDE) * 2
        for source, which in ((weight, core), (other, 1 - core)):
            start = pl.multiple_of((holder + which) * span, span)
            full[pl.ds(start, span)] = source[item * span : (item + 1) * span]


def project_kernel(mixed, stats, upper, full, *refs):
    projected, merged = refs[-2:]
    largest, total = stats[:HEADS], stats[HEADS:]
    parts = upper[CHANNELS : CHANNELS + 32].astype(jnp.float32)
    lse = parts[:HEADS] + parts[HEADS : 2 * HEADS] + parts[2 * HEADS : 3 * HEADS]
    lse = jnp.where(lax.axis_index("row") > 0, lse, jnp.float32(NEG))
    top = jnp.maximum(largest, lse)
    own_w = jnp.exp2(largest - top)
    upper_w = jnp.exp2(lse - top)
    share = 1.0 / (total * own_w + upper_w)
    own_w, upper_w = own_w * share, upper_w * share
    for head in range(HEADS):
        rows = slice(head * HDIM, (head + 1) * HDIM)
        merged[rows] = (
            mixed[rows] * own_w[head : head + 1]
            + upper[rows].astype(jnp.float32) * upper_w[head : head + 1]
        ).astype(jnp.bfloat16)
    result = lax.dot_general(
        merged[...].T, full[...], (((1,), (1,)), ((), ())), preferred_element_type=jnp.float32
    )
    projected[...] = result.astype(jnp.bfloat16).reshape(projected.shape)


def call(kernel, outs, scratch=(), flops=0, name=None, **more):
    return pl.pallas_call(
        kernel,
        out_shape=outs,
        scratch_shapes=list(scratch),
        compiler_params=pltpu.CompilerParams(vmem_limit_bytes=32 * 1024 * 1024),
        cost_estimate=pl.CostEstimate(flops=flops, bytes_accessed=1024, transcendentals=0),
        name=name,
        **more,
    )


STACK_FLOPS = 6_000_000_000
OWN_FLOPS = 1024
PAIR_FLOPS = 1024
PART_FLOPS = 1024


def own_part(col, query, pair_a, pair_b):
    return call(
        functools.partial(own_kernel, col),
        (
            jax.ShapeDtypeStruct((CHANNELS, TOKENS), jnp.float32),
            jax.ShapeDtypeStruct((2 * HEADS, TOKENS), jnp.float32),
        ),
        flops=OWN_FLOPS if col else 1024, name=f"own_{col}",
    )(query, pair_a, pair_b)


def upper_part(col, query, pair_a, pair_b, *earlier):
    def kernel(query, pair_a, pair_b, *refs):
        part_kernel(col, query, pair_a, pair_b, *refs[-2:])

    whole = pl.BlockSpec(memory_space=pltpu.VMEM)
    return call(
        kernel,
        jax.ShapeDtypeStruct((PACKED, TOKENS), jnp.bfloat16),
        (pltpu.VMEM((HEADS, TOKENS), jnp.float32),),
        flops=PART_FLOPS, name=f"part_{col}",
        in_specs=[whole] * 3 + [pl.BlockSpec(memory_space=pl.ANY)] * len(earlier),
    )(query, pair_a, pair_b, *earlier)


def project(col, own, upper, full, shape, before=None):
    whole = lambda a: pl.BlockSpec(a.shape, lambda i: (0,) * a.ndim)
    operands = [*own, upper, full]
    specs = [whole(a) for a in operands]
    aliases = {}
    if before is not None:
        aliases = {len(operands): 0}
        operands.append(before)
        specs.append(pl.BlockSpec(memory_space=pl.ANY))
    return call(
        project_kernel,
        jax.ShapeDtypeStruct(shape, jnp.bfloat16),
        (pltpu.VMEM((CHANNELS, TOKENS), jnp.bfloat16),),
        flops=1024, name=f"project_{col}",
        grid=(1,), in_specs=specs,
        out_specs=pl.BlockSpec((BLOCK, BLOCK, shape[2]), lambda i: (0, col, 0)),
        input_output_aliases=aliases,
    )(*operands)


def from_part(block, distance):
    return routed(
        block, range(SIDE), lambda x, zh, c, y: (x, (zh - distance) % SIDE, c, y)
    )


def weight_both(half, members):
    other = routed(half, members, lambda x, zh, c, y: (x, zh, 1 - c, y))
    return call(
        order_kernel, jax.ShapeDtypeStruct((2 * half.shape[0], half.shape[1]), half.dtype), name="order"
    )(half, other)


def after(value, *others):
    return lax.optimization_barrier((value, *others))[0]


def outputs(own_1, own_0, upper_1, upper_0, full, query):
    shape = (query.shape[0], query.shape[1], full.shape[0])
    right = project(1, own_1, upper_1, full, shape)
    return project(0, own_0, upper_0, full, shape, right)


def by_frame(late, early, *operands):
    z_lo = lax.rem(lax.axis_index("frame"), SIDE)
    half = SIDE // 2
    return lax.cond(
        z_lo < half,
        functools.partial(late, range(half)),
        functools.partial(early, range(half, SIDE)),
        *operands,
    )


def on_device(query, keys, values, out_weight):
    frames = range(SIDE)
    shard = out_weight.T
    following = from_part(shard, 1)
    previous = from_part(shard, -1)
    lower_query = routed(query, frames, to_row(-1))
    pair_0, pair_1 = call(
        pair_kernel,
        [jax.ShapeDtypeStruct((2 * BLOCK, BLOCK, CHANNELS), jnp.bfloat16)] * 2,
        flops=PAIR_FLOPS, name="pair",
    )(keys, values)
    left = routed(pair_1, frames, to_right)
    own_1 = own_part(1, query, pair_0, pair_1)
    previous = after(previous, following, own_1[1])
    far = from_part(previous, -1)
    items = call(
        stack_kernel, jax.ShapeDtypeStruct((SIDE, *shard.shape), shard.dtype),
        flops=STACK_FLOPS, name="stack",
    )(shard, following, far, previous)

    def gather(items):
        half = lax.all_gather(items, "col", axis=1, tiled=True)
        return half.reshape(-1, half.shape[2])

    def first_late(members, items):
        return gather(items)

    def first_early(members, items):
        return jnp.zeros((SIDE * SIDE * items.shape[1], CHANNELS), items.dtype)

    half = by_frame(first_late, first_early, items)
    part_1 = upper_part(1, lower_query, pair_0, pair_1, half)
    upper_1 = routed(part_1, frames, to_row(1))
    part_0 = upper_part(0, lower_query, left, pair_0, part_1)
    upper_0 = routed(part_0, frames, to_row(1))

    def last_late(members, items, half, query, left, pair_0):
        return weight_both(half, members), *own_part(0, query, left, pair_0)

    def last_early(members, items, half, query, left, pair_0):
        own_0 = own_part(0, query, left, pair_0)
        return weight_both(gather(after(items, own_0[1])), members), *own_0

    full, *own_0 = by_frame(
        last_late, last_early, after(items, part_0), half, query, left, pair_0
    )
    return outputs(own_1, own_0, upper_1, upper_0, full, query)


def solution(mesh):
    placed = (
        P(("frame", "row"), "col", None),
        P(("frame", "row"), "col", None),
        P(("frame", "row"), "col", None),
        P(None, ("row", "col")),
    )
    return jax.shard_map(
        on_device,
        mesh=mesh,
        in_specs=placed,
        out_specs=P(("frame", "row"), "col", None),
        check_vma=False,
    )
```

```python
import functools
import math

import jax
import jax.numpy as jnp
from jax import lax
from jax.experimental import pallas as pl
from jax.experimental.pallas import tpu as pltpu
from jax.sharding import PartitionSpec as P

HEADS = 8
HDIM = 80
BLOCK = 16
TOKENS = BLOCK * BLOCK
CHANNELS = HEADS * HDIM
SCALE = math.log2(math.e) * HDIM ** (-0.5)
NEG = -1e30
PACKED = CHANNELS + 32
SIDE = 4
AXES = ("frame", "row", "col")


def place(x, zl, zh, core, y):
    return ((x * SIDE + zl) * 2 * SIDE + zh * 2 + core) * SIDE + y


def routed(block, members, target):
    route = []
    for x in range(SIDE):
        for zl in members:
            for zh in range(SIDE):
                for core in range(2):
                    for y in range(SIDE):
                        to = target(x, zh, core, y)
                        if to is not None:
                            route.append((place(x, zl, zh, core, y), place(to[0], zl, *to[1:])))
    return lax.ppermute(block, AXES, route)


def to_row(distance):
    def target(x, zh, core, y):
        row = zh * 2 + core + distance
        return (x, row // 2, row % 2, y) if 0 <= row < 2 * SIDE else None

    return target


def to_right(x, zh, core, y):
    return (x, zh, core, y + 1) if y + 1 < SIDE else None


def head_scores(keys, query_t, head):
    first = head * HDIM
    low = first // 128 * 128
    high = -(-(first + HDIM) // 128) * 128
    parts = []
    if first > low:
        parts.append(jnp.zeros((first - low, TOKENS), jnp.bfloat16))
    parts.append(query_t[first : first + HDIM])
    if high > first + HDIM:
        parts.append(jnp.zeros((high - first - HDIM, TOKENS), jnp.bfloat16))
    masked = jnp.concatenate(parts, axis=0)
    return jnp.dot(keys[:, low:high], masked, preferred_element_type=jnp.float32)


def attend(query_t, pair_a, pair_b, bias, emit):
    keys_a, keys_b = (p[:BLOCK].reshape(TOKENS, CHANNELS) for p in (pair_a, pair_b))
    values_a, values_b = (p[BLOCK:].reshape(TOKENS, CHANNELS).T for p in (pair_a, pair_b))
    for head in range(HEADS):
        rows = slice(head * HDIM, (head + 1) * HDIM)
        score_a = head_scores(keys_a, query_t, head)
        score_b = head_scores(keys_b, query_t, head)
        if bias is not None:
            score_a = score_a + bias
        largest = jnp.maximum(
            jnp.max(score_a, axis=0, keepdims=True), jnp.max(score_b, axis=0, keepdims=True)
        )
        largest = largest * SCALE
        weight_a = jnp.exp2(score_a * SCALE - largest)
        weight_b = jnp.exp2(score_b * SCALE - largest)
        total = jnp.sum(weight_a, axis=0, keepdims=True) + jnp.sum(weight_b, axis=0, keepdims=True)
        mixed = jnp.dot(
            values_a[rows], weight_a.astype(jnp.bfloat16), preferred_element_type=jnp.float32
        ) + jnp.dot(
            values_b[rows], weight_b.astype(jnp.bfloat16), preferred_element_type=jnp.float32
        )
        emit(head, rows, mixed, largest, total)


def block_of(ref, col):
    return ref[:, col * BLOCK : (col + 1) * BLOCK, :].reshape(TOKENS, CHANNELS)


def edge_bias(col):
    if col > 0:
        return None
    return jnp.where(lax.axis_index("col") > 0, jnp.float32(0.0), jnp.float32(NEG))


def pair_kernel(keys, values, pair_0, pair_1):
    for col, pair in ((0, pair_0), (1, pair_1)):
        pair[:BLOCK] = keys[:, col * BLOCK : (col + 1) * BLOCK]
        pair[BLOCK:] = values[:, col * BLOCK : (col + 1) * BLOCK]


def stack_kernel(*refs):
    for j, ref in enumerate(refs[:-1]):
        refs[-1][j] = ref[...]


def own_kernel(col, query, pair_a, pair_b, mixed_out, stats_out):
    def emit(head, rows, mixed, largest, total):
        mixed_out[rows] = mixed
        stats_out[head : head + 1] = largest
        stats_out[HEADS + head : HEADS + head + 1] = total

    attend(block_of(query, col).T, pair_a, pair_b, edge_bias(col), emit)


def part_kernel(col, query, pair_a, pair_b, packed, lse):
    def emit(head, rows, mixed, largest, total):
        packed[rows] = (mixed * (1.0 / total)).astype(jnp.bfloat16)
        lse[head : head + 1] = largest + jnp.log2(total)

    attend(block_of(query, col).T, pair_a, pair_b, edge_bias(col), emit)
    whole = lse[...]
    high = whole.astype(jnp.bfloat16).astype(jnp.float32)
    middle = (whole - high).astype(jnp.bfloat16).astype(jnp.float32)
    low = whole - high - middle
    packed[CHANNELS : CHANNELS + 16] = jnp.concatenate([high, middle], axis=0).astype(jnp.bfloat16)
    packed[CHANNELS + 16 : CHANNELS + 32] = jnp.concatenate(
        [low, jnp.zeros_like(whole)], axis=0
    ).astype(jnp.bfloat16)


def order_kernel(weight, other, full):
    row = lax.axis_index("row")
    z_hi, core = row // 2, row % 2
    span = full.shape[0] // (2 * SIDE)
    for item in range(SIDE):
        holder = lax.rem(z_hi + item, SIDE) * 2
        for source, which in ((weight, core), (other, 1 - core)):
            start = pl.multiple_of((holder + which) * span, span)
            full[pl.ds(start, span)] = source[item * span : (item + 1) * span]


def project_kernel(mixed, stats, upper, full, *refs):
    projected, merged = refs[-2:]
    largest, total = stats[:HEADS], stats[HEADS:]
    parts = upper[CHANNELS : CHANNELS + 32].astype(jnp.float32)
    lse = parts[:HEADS] + parts[HEADS : 2 * HEADS] + parts[2 * HEADS : 3 * HEADS]
    lse = jnp.where(lax.axis_index("row") > 0, lse, jnp.float32(NEG))
    top = jnp.maximum(largest, lse)
    own_w = jnp.exp2(largest - top)
    upper_w = jnp.exp2(lse - top)
    share = 1.0 / (total * own_w + upper_w)
    own_w, upper_w = own_w * share, upper_w * share
    for head in range(HEADS):
        rows = slice(head * HDIM, (head + 1) * HDIM)
        merged[rows] = (
            mixed[rows] * own_w[head : head + 1]
            + upper[rows].astype(jnp.float32) * upper_w[head : head + 1]
        ).astype(jnp.bfloat16)
    result = lax.dot_general(
        merged[...].T, full[...], (((1,), (1,)), ((), ())), preferred_element_type=jnp.float32
    )
    projected[...] = result.astype(jnp.bfloat16).reshape(projected.shape)


def call(kernel, outs, scratch=(), flops=0, name=None, **more):
    return pl.pallas_call(
        kernel,
        out_shape=outs,
        scratch_shapes=list(scratch),
        compiler_params=pltpu.CompilerParams(vmem_limit_bytes=32 * 1024 * 1024),
        cost_estimate=pl.CostEstimate(flops=flops, bytes_accessed=1024, transcendentals=0),
        name=name,
        **more,
    )


STACK_FLOPS = 6_000_000_000
OWN_FLOPS = 1024
PAIR_FLOPS = 1024
PART_FLOPS = 1024


def own_part(col, query, pair_a, pair_b):
    return call(
        functools.partial(own_kernel, col),
        (
            jax.ShapeDtypeStruct((CHANNELS, TOKENS), jnp.float32),
            jax.ShapeDtypeStruct((2 * HEADS, TOKENS), jnp.float32),
        ),
        flops=OWN_FLOPS if col else 1024, name=f"own_{col}",
    )(query, pair_a, pair_b)


def upper_part(col, query, pair_a, pair_b, *earlier):
    def kernel(query, pair_a, pair_b, *refs):
        part_kernel(col, query, pair_a, pair_b, *refs[-2:])

    whole = pl.BlockSpec(memory_space=pltpu.VMEM)
    return call(
        kernel,
        jax.ShapeDtypeStruct((PACKED, TOKENS), jnp.bfloat16),
        (pltpu.VMEM((HEADS, TOKENS), jnp.float32),),
        flops=PART_FLOPS, name=f"part_{col}",
        in_specs=[whole] * 3 + [pl.BlockSpec(memory_space=pl.ANY)] * len(earlier),
    )(query, pair_a, pair_b, *earlier)


def project(col, own, upper, full, shape, before=None):
    whole = lambda a: pl.BlockSpec(a.shape, lambda i: (0,) * a.ndim)
    operands = [*own, upper, full]
    specs = [whole(a) for a in operands]
    aliases = {}
    if before is not None:
        aliases = {len(operands): 0}
        operands.append(before)
        specs.append(pl.BlockSpec(memory_space=pl.ANY))
    return call(
        project_kernel,
        jax.ShapeDtypeStruct(shape, jnp.bfloat16),
        (pltpu.VMEM((CHANNELS, TOKENS), jnp.bfloat16),),
        flops=1024, name=f"project_{col}",
        grid=(1,), in_specs=specs,
        out_specs=pl.BlockSpec((BLOCK, BLOCK, shape[2]), lambda i: (0, col, 0)),
        input_output_aliases=aliases,
    )(*operands)


def from_part(block, distance):
    return routed(
        block, range(SIDE), lambda x, zh, c, y: (x, (zh - distance) % SIDE, c, y)
    )


def weight_both(half, members):
    other = routed(half, members, lambda x, zh, c, y: (x, zh, 1 - c, y))
    return call(
        order_kernel, jax.ShapeDtypeStruct((2 * half.shape[0], half.shape[1]), half.dtype), name="order"
    )(half, other)


def after(value, *others):
    return lax.optimization_barrier((value, *others))[0]


def outputs(own_1, own_0, upper_1, upper_0, full, query):
    shape = (query.shape[0], query.shape[1], full.shape[0])
    right = project(1, own_1, upper_1, full, shape)
    return project(0, own_0, upper_0, full, shape, right)


def by_frame(late, early, *operands):
    z_lo = lax.rem(lax.axis_index("frame"), SIDE)
    half = SIDE // 2
    return lax.cond(
        z_lo < half,
        functools.partial(late, range(half)),
        functools.partial(early, range(half, SIDE)),
        *operands,
    )


def on_device(query, keys, values, out_weight):
    frames = range(SIDE)
    shard = out_weight.T
    following = from_part(shard, 1)
    previous = from_part(shard, -1)
    lower_query = routed(query, frames, to_row(-1))
    pair_0, pair_1 = call(
        pair_kernel,
        [jax.ShapeDtypeStruct((2 * BLOCK, BLOCK, CHANNELS), jnp.bfloat16)] * 2,
        flops=PAIR_FLOPS, name="pair",
    )(keys, values)
    left = routed(pair_1, frames, to_right)
    previous = after(previous, following, pair_1)
    far = from_part(previous, -1)
    own_1 = own_part(1, query, pair_0, pair_1)
    items = call(
        stack_kernel, jax.ShapeDtypeStruct((SIDE, *shard.shape), shard.dtype),
        flops=STACK_FLOPS, name="stack",
    )(shard, following, after(far, own_1[1]), previous)

    def gather(items):
        half = lax.all_gather(items, "col", axis=1, tiled=True)
        return half.reshape(-1, half.shape[2])

    def first_late(members, items):
        return gather(items)

    def first_early(members, items):
        return jnp.zeros((SIDE * SIDE * items.shape[1], CHANNELS), items.dtype)

    half = by_frame(first_late, first_early, items)
    part_1 = upper_part(1, lower_query, pair_0, pair_1, half)
    upper_1 = routed(part_1, frames, to_row(1))
    part_0 = upper_part(0, lower_query, left, pair_0, part_1)
    upper_0 = routed(part_0, frames, to_row(1))

    def last_late(members, items, half, query, left, pair_0):
        return weight_both(half, members), *own_part(0, query, left, pair_0)

    def last_early(members, items, half, query, left, pair_0):
        half = gather(items)
        return weight_both(half, members), *own_part(0, after(query, half), left, pair_0)

    full, *own_0 = by_frame(
        last_late, last_early, after(items, part_0), half, query, left, pair_0
    )
    return outputs(own_1, own_0, upper_1, upper_0, full, query)


def solution(mesh):
    placed = (
        P(("frame", "row"), "col", None),
        P(("frame", "row"), "col", None),
        P(("frame", "row"), "col", None),
        P(None, ("row", "col")),
    )
    return jax.shard_map(
        on_device,
        mesh=mesh,
        in_specs=placed,
        out_specs=P(("frame", "row"), "col", None),
        check_vma=False,
    )
```

```python
import functools
import math

import jax
import jax.numpy as jnp
from jax import lax
from jax.experimental import pallas as pl
from jax.experimental.pallas import tpu as pltpu
from jax.sharding import PartitionSpec as P

HEADS = 8
HDIM = 80
BLOCK = 16
TOKENS = BLOCK * BLOCK
CHANNELS = HEADS * HDIM
SCALE = math.log2(math.e) * HDIM ** (-0.5)
NEG = -1e30
PACKED = CHANNELS + 32
SIDE = 4
AXES = ("frame", "row", "col")


def place(x, zl, zh, core, y):
    return ((x * SIDE + zl) * 2 * SIDE + zh * 2 + core) * SIDE + y


def routed(block, members, target):
    route = []
    for x in range(SIDE):
        for zl in members:
            for zh in range(SIDE):
                for core in range(2):
                    for y in range(SIDE):
                        to = target(x, zh, core, y)
                        if to is not None:
                            route.append((place(x, zl, zh, core, y), place(to[0], zl, *to[1:])))
    return lax.ppermute(block, AXES, route)


def to_row(distance):
    def target(x, zh, core, y):
        row = zh * 2 + core + distance
        return (x, row // 2, row % 2, y) if 0 <= row < 2 * SIDE else None

    return target


def to_right(x, zh, core, y):
    return (x, zh, core, y + 1) if y + 1 < SIDE else None


def head_scores(keys, query_t, head):
    first = head * HDIM
    low = first // 128 * 128
    high = -(-(first + HDIM) // 128) * 128
    parts = []
    if first > low:
        parts.append(jnp.zeros((first - low, TOKENS), jnp.bfloat16))
    parts.append(query_t[first : first + HDIM])
    if high > first + HDIM:
        parts.append(jnp.zeros((high - first - HDIM, TOKENS), jnp.bfloat16))
    masked = jnp.concatenate(parts, axis=0)
    return jnp.dot(keys[:, low:high], masked, preferred_element_type=jnp.float32)


def attend(query_t, pair_a, pair_b, bias, emit):
    keys_a, keys_b = (p[:BLOCK].reshape(TOKENS, CHANNELS) for p in (pair_a, pair_b))
    values_a, values_b = (p[BLOCK:].reshape(TOKENS, CHANNELS).T for p in (pair_a, pair_b))
    for head in range(HEADS):
        rows = slice(head * HDIM, (head + 1) * HDIM)
        score_a = head_scores(keys_a, query_t, head)
        score_b = head_scores(keys_b, query_t, head)
        if bias is not None:
            score_a = score_a + bias
        largest = jnp.maximum(
            jnp.max(score_a, axis=0, keepdims=True), jnp.max(score_b, axis=0, keepdims=True)
        )
        largest = largest * SCALE
        weight_a = jnp.exp2(score_a * SCALE - largest)
        weight_b = jnp.exp2(score_b * SCALE - largest)
        total = jnp.sum(weight_a, axis=0, keepdims=True) + jnp.sum(weight_b, axis=0, keepdims=True)
        mixed = jnp.dot(
            values_a[rows], weight_a.astype(jnp.bfloat16), preferred_element_type=jnp.float32
        ) + jnp.dot(
            values_b[rows], weight_b.astype(jnp.bfloat16), preferred_element_type=jnp.float32
        )
        emit(head, rows, mixed, largest, total)


def block_of(ref, col):
    return ref[:, col * BLOCK : (col + 1) * BLOCK, :].reshape(TOKENS, CHANNELS)


def edge_bias(col):
    if col > 0:
        return None
    return jnp.where(lax.axis_index("col") > 0, jnp.float32(0.0), jnp.float32(NEG))


def pair_kernel(keys, values, pair_0, pair_1):
    for col, pair in ((0, pair_0), (1, pair_1)):
        pair[:BLOCK] = keys[:, col * BLOCK : (col + 1) * BLOCK]
        pair[BLOCK:] = values[:, col * BLOCK : (col + 1) * BLOCK]


def stack_kernel(*refs):
    for j, ref in enumerate(refs[:-1]):
        refs[-1][j] = ref[...]


def own_kernel(col, query, pair_a, pair_b, mixed_out, stats_out):
    def emit(head, rows, mixed, largest, total):
        mixed_out[rows] = mixed
        stats_out[head : head + 1] = largest
        stats_out[HEADS + head : HEADS + head + 1] = total

    attend(block_of(query, col).T, pair_a, pair_b, edge_bias(col), emit)


def part_kernel(col, query, pair_a, pair_b, packed, lse):
    def emit(head, rows, mixed, largest, total):
        packed[rows] = (mixed * (1.0 / total)).astype(jnp.bfloat16)
        lse[head : head + 1] = largest + jnp.log2(total)

    attend(block_of(query, col).T, pair_a, pair_b, edge_bias(col), emit)
    whole = lse[...]
    high = whole.astype(jnp.bfloat16).astype(jnp.float32)
    middle = (whole - high).astype(jnp.bfloat16).astype(jnp.float32)
    low = whole - high - middle
    packed[CHANNELS : CHANNELS + 16] = jnp.concatenate([high, middle], axis=0).astype(jnp.bfloat16)
    packed[CHANNELS + 16 : CHANNELS + 32] = jnp.concatenate(
        [low, jnp.zeros_like(whole)], axis=0
    ).astype(jnp.bfloat16)


def order_kernel(weight, other, full):
    row = lax.axis_index("row")
    z_hi, core = row // 2, row % 2
    span = full.shape[0] // (2 * SIDE)
    for item in range(SIDE):
        holder = lax.rem(z_hi + item, SIDE) * 2
        for source, which in ((weight, core), (other, 1 - core)):
            start = pl.multiple_of((holder + which) * span, span)
            full[pl.ds(start, span)] = source[item * span : (item + 1) * span]


def project_kernel(mixed, stats, upper, full, *refs):
    projected, merged = refs[-2:]
    largest, total = stats[:HEADS], stats[HEADS:]
    parts = upper[CHANNELS : CHANNELS + 32].astype(jnp.float32)
    lse = parts[:HEADS] + parts[HEADS : 2 * HEADS] + parts[2 * HEADS : 3 * HEADS]
    lse = jnp.where(lax.axis_index("row") > 0, lse, jnp.float32(NEG))
    top = jnp.maximum(largest, lse)
    own_w = jnp.exp2(largest - top)
    upper_w = jnp.exp2(lse - top)
    share = 1.0 / (total * own_w + upper_w)
    own_w, upper_w = own_w * share, upper_w * share
    for head in range(HEADS):
        rows = slice(head * HDIM, (head + 1) * HDIM)
        merged[rows] = (
            mixed[rows] * own_w[head : head + 1]
            + upper[rows].astype(jnp.float32) * upper_w[head : head + 1]
        ).astype(jnp.bfloat16)
    result = lax.dot_general(
        merged[...].T, full[...], (((1,), (1,)), ((), ())), preferred_element_type=jnp.float32
    )
    projected[...] = result.astype(jnp.bfloat16).reshape(projected.shape)


def call(kernel, outs, scratch=(), flops=0, name=None, **more):
    return pl.pallas_call(
        kernel,
        out_shape=outs,
        scratch_shapes=list(scratch),
        compiler_params=pltpu.CompilerParams(vmem_limit_bytes=20 * 1024 * 1024),
        cost_estimate=pl.CostEstimate(flops=flops, bytes_accessed=1024, transcendentals=0),
        name=name,
        **more,
    )


STACK_FLOPS = 6_000_000_000
OWN_FLOPS = 1024
PAIR_FLOPS = 1024
PART_FLOPS = 1024


def own_part(col, query, pair_a, pair_b):
    return call(
        functools.partial(own_kernel, col),
        (
            jax.ShapeDtypeStruct((CHANNELS, TOKENS), jnp.float32),
            jax.ShapeDtypeStruct((2 * HEADS, TOKENS), jnp.float32),
        ),
        flops=OWN_FLOPS if col else 1024, name=f"own_{col}",
    )(query, pair_a, pair_b)


def upper_part(col, query, pair_a, pair_b, *earlier):
    def kernel(query, pair_a, pair_b, *refs):
        part_kernel(col, query, pair_a, pair_b, *refs[-2:])

    whole = pl.BlockSpec(memory_space=pltpu.VMEM)
    return call(
        kernel,
        jax.ShapeDtypeStruct((PACKED, TOKENS), jnp.bfloat16),
        (pltpu.VMEM((HEADS, TOKENS), jnp.float32),),
        flops=PART_FLOPS, name=f"part_{col}",
        in_specs=[whole] * 3 + [pl.BlockSpec(memory_space=pl.ANY)] * len(earlier),
    )(query, pair_a, pair_b, *earlier)


def project(col, own, upper, full, shape, before=None):
    whole = lambda a: pl.BlockSpec(a.shape, lambda i: (0,) * a.ndim)
    operands = [*own, upper, full]
    specs = [whole(a) for a in operands]
    aliases = {}
    if before is not None:
        aliases = {len(operands): 0}
        operands.append(before)
        specs.append(pl.BlockSpec(memory_space=pl.ANY))
    return call(
        project_kernel,
        jax.ShapeDtypeStruct(shape, jnp.bfloat16),
        (pltpu.VMEM((CHANNELS, TOKENS), jnp.bfloat16),),
        flops=1024, name=f"project_{col}",
        grid=(1,), in_specs=specs,
        out_specs=pl.BlockSpec((BLOCK, BLOCK, shape[2]), lambda i: (0, col, 0)),
        input_output_aliases=aliases,
    )(*operands)


def from_part(block, distance):
    return routed(
        block, range(SIDE), lambda x, zh, c, y: (x, (zh - distance) % SIDE, c, y)
    )


def weight_both(half, members):
    other = routed(half, members, lambda x, zh, c, y: (x, zh, 1 - c, y))
    return call(
        order_kernel, jax.ShapeDtypeStruct((2 * half.shape[0], half.shape[1]), half.dtype), name="order"
    )(half, other)


def after(value, *others):
    return lax.optimization_barrier((value, *others))[0]


def outputs(own_1, own_0, upper_1, upper_0, full, query):
    shape = (query.shape[0], query.shape[1], full.shape[0])
    right = project(1, own_1, upper_1, full, shape)
    return project(0, own_0, upper_0, full, shape, right)


def by_frame(late, early, *operands):
    z_lo = lax.rem(lax.axis_index("frame"), SIDE)
    half = SIDE // 2
    return lax.cond(
        z_lo < half,
        functools.partial(late, range(half)),
        functools.partial(early, range(half, SIDE)),
        *operands,
    )


def on_device(query, keys, values, out_weight):
    frames = range(SIDE)
    shard = out_weight.T
    following = from_part(shard, 1)
    previous = from_part(shard, -1)
    lower_query = routed(query, frames, to_row(-1))
    pair_0, pair_1 = call(
        pair_kernel,
        [jax.ShapeDtypeStruct((2 * BLOCK, BLOCK, CHANNELS), jnp.bfloat16)] * 2,
        flops=PAIR_FLOPS, name="pair",
    )(keys, values)
    left = routed(pair_1, frames, to_right)
    previous = after(previous, following, pair_1)
    far = from_part(previous, -1)
    own_1 = own_part(1, query, pair_0, pair_1)
    items = call(
        stack_kernel, jax.ShapeDtypeStruct((SIDE, *shard.shape), shard.dtype),
        flops=STACK_FLOPS, name="stack",
    )(shard, following, after(far, own_1[1]), previous)

    def gather(items):
        half = lax.all_gather(items, "col", axis=1, tiled=True)
        return half.reshape(-1, half.shape[2])

    def first_late(members, items):
        return gather(items)

    def first_early(members, items):
        return jnp.zeros((SIDE * SIDE * items.shape[1], CHANNELS), items.dtype)

    half = by_frame(first_late, first_early, items)
    part_1 = upper_part(1, lower_query, pair_0, pair_1, half)
    upper_1 = routed(part_1, frames, to_row(1))
    part_0 = upper_part(0, lower_query, left, pair_0, part_1)
    upper_0 = routed(part_0, frames, to_row(1))

    def last_late(members, items, half, query, left, pair_0):
        return weight_both(half, members), *own_part(0, query, left, pair_0)

    def last_early(members, items, half, query, left, pair_0):
        half = gather(items)
        return weight_both(half, members), *own_part(0, after(query, half), left, pair_0)

    full, *own_0 = by_frame(
        last_late, last_early, after(items, part_0), half, query, left, pair_0
    )
    return outputs(own_1, own_0, upper_1, upper_0, full, query)


def solution(mesh):
    placed = (
        P(("frame", "row"), "col", None),
        P(("frame", "row"), "col", None),
        P(("frame", "row"), "col", None),
        P(None, ("row", "col")),
    )
    return jax.shard_map(
        on_device,
        mesh=mesh,
        in_specs=placed,
        out_specs=P(("frame", "row"), "col", None),
        check_vma=False,
    )
```
